128 devices in a mesh: group: 16 (over x, y_hi, core), tensor: 8 (over y_lo, z).
Axes of the slice: x: 4, y: 4 (y_hi: 2, y_lo: 2; y = y_hi * 2 + y_lo), z: 4, core: 2. Of those that a mesh axis runs over, the one named last changes fastest.
Arguments:
- completion_query_slots: bfloat16 [8192, 8192], P('group', 'tensor'), may hold values from -8 to 8
- completion_key_array: bfloat16 [8192, 1024], P('group', 'tensor'), may hold values from -6 to 6
- completion_value_array: bfloat16 [8192, 1024], P('group', 'tensor'), may hold values from -6 to 6
- comp_dout: bfloat16 [8192, 8192], P('group', 'tensor'), may hold values from -192 to 192
- prompt_query_array: bfloat16 [1536, 8192], P('group', 'tensor'), may hold values from -8 to 8
- prompt_key_array: bfloat16 [1536, 1024], P('group', 'tensor'), may hold values from -8 to 8
- prompt_value_array: bfloat16 [1536, 1024], P('group', 'tensor'), may hold values from -6 to 6
- prompt_output_cotangent: bfloat16 [1536, 8192], P('group', 'tensor'), may hold values from -48 to 48
- lengths: int32 [16], replicated, may hold values from 1 to 4, 40 in all
- slot_of: int32 [16], replicated, may hold values from 0 to 15, each once
- passes: int32 [16, 32], P('group', 'tensor'), may hold values from 0 to 1
Outputs:
- comp_dq: bfloat16 [8192, 8192], P('group', 'tensor')
- completion_key_gradients: bfloat16 [8192, 1024], P('group', 'tensor')
- completion_value_gradients: bfloat16 [8192, 1024], P('group', 'tensor')
- prompt_dq: bfloat16 [1536, 8192], P('group', 'tensor')
- prompt_key_gradients: bfloat16 [1536, 1024], P('group', 'tensor')
- prompt_value_gradients: bfloat16 [1536, 1024], P('group', 'tensor')
The draws below stay inside these ranges and needn't reach their ends.
Inputs may be any that keep to these rules, and one draw needn't show every extreme that they name: `lengths`: counts in blocks of 128 tokens; they sum to 40 and the longest completion has exactly 4 blocks. `slot_of`: each slot holds exactly one completion.
All inputs are finite; a program needn't handle non-finite values.
Results may differ from the reference program's by a relative error of at most 0.008.
Values may be sent and summed in bfloat16 or wider, within the bound.
A program may use at most 64 MiB of HBM per device.

```python
import math
import jax
import jax.numpy as jnp
import numpy as np
from jax import lax

QUERY_HEADS = 64
KEY_VALUE_HEADS = 8
HEAD_SIZE = 128
BLK = 128
MAXB = 4
TESTS = 32
COMPLETION_COUNT = 16
COMPLETION_SLOTS = 512
PROMPT_TOKENS = 1536


def draw_prompt_key_array(key, part):
    key = jax.random.fold_in(key, 3)
    sampled_values = jnp.clip(jax.random.normal(key, (PROMPT_TOKENS, KEY_VALUE_HEADS * HEAD_SIZE), jnp.float32), -6.0, 6.0)
    return sampled_values.astype(jnp.bfloat16)


def draw_prompt_query_array(key, part):
    key = jax.random.fold_in(key, 7)
    sampled_values = jnp.clip(jax.random.normal(key, (PROMPT_TOKENS, QUERY_HEADS * HEAD_SIZE), jnp.float32), -6.0, 6.0)
    return sampled_values.astype(jnp.bfloat16)


def draw_completion_query_slots(key, part):
    key = jax.random.fold_in(key, 9)
    sampled_values = jnp.clip(jax.random.normal(key, (COMPLETION_COUNT * COMPLETION_SLOTS, QUERY_HEADS * HEAD_SIZE), jnp.float32), -6.0, 6.0)
    return sampled_values.astype(jnp.bfloat16)


def draw_passes(key, part):
    key = jax.random.fold_in(key, 5)
    first_key, second_key = jax.random.split(key)
    levels = jax.random.randint(first_key, (COMPLETION_COUNT, 1), 100, 900)
    rolls_drawn = jax.random.randint(second_key, (COMPLETION_COUNT, TESTS), 0, 1000)
    return (rolls_drawn < levels).astype(jnp.int32)


def level_of(key, dims, pieces, smallest, top_value):
    def one(position, parts):
        heights = jax.random.uniform(jax.random.fold_in(jax.random.fold_in(key, 6), position), (parts,), jnp.float32, smallest / len(pieces), top_value / len(pieces))
        return jnp.repeat(jnp.exp(heights), dims[position] // parts).reshape((-1,) + (1,) * (len(dims) - position - 1))

    factor_of = one(*pieces[0])
    for cut in pieces[1:]:
        factor_of = factor_of * one(*cut)
    return factor_of


def split_up(count, total, limit, slope):
    loads = [(1 << 20) // math.isqrt(standing ** slope) + 1 for standing in range(2, count + 1)]
    surplus, given = total - limit - (count - 1), [1] * (count - 1)
    while surplus > 0:
        free = [i for i in range(count - 1) if given[i] < limit]
        whole, remaining = sum([loads[i] for i in free]), surplus
        for i in free:
            addition = min(limit - given[i], max(1, remaining * loads[i] // whole), surplus)
            given[i] = given[i] + addition
            surplus = surplus - addition
    return np.array([limit] + given)


def uneven(key, number_of, total, bound, lean):
    if number_of == 2:
        one = jax.random.randint(key, (), max(1, total - bound), min(bound, total - 1) + 1)
        return jnp.stack([one, total - one])
    sizes = jnp.asarray(split_up(number_of, total, bound, lean), jnp.int32)
    pairs = (number_of - 1) // 2
    source_of, receiver = sizes[1:1 + 2 * pairs:2], sizes[2:2 + 2 * pairs:2]
    room = jnp.minimum(source_of - 1, bound - receiver)
    passed = jax.random.randint(jax.random.fold_in(key, 1), (pairs,), 0, 1 << 20) % (room + 1)
    sizes = sizes.at[1:1 + 2 * pairs:2].set(source_of - passed).at[2:2 + 2 * pairs:2].set(receiver + passed)
    return sizes[jax.random.permutation(jax.random.fold_in(key, 2), number_of)]


def noise(key, dims, deviation, limit, pieces=(), kind=jnp.bfloat16):
    drawn = deviation * jax.random.normal(key, dims, jnp.float32)
    if pieces:
        drawn = drawn * level_of(key, dims, pieces, -0.22, 0.18)
    return jnp.clip(drawn, -limit, limit).astype(kind)


def setup_inputs(seed: int = 0) -> dict:
    key_of = jax.random.split(jax.random.key(seed), 12)
    return {
        "completion_query_slots": draw_completion_query_slots(jax.random.fold_in(key_of[11], 71), 0),
        "completion_key_array": noise(key_of[1], (COMPLETION_COUNT * COMPLETION_SLOTS, KEY_VALUE_HEADS * HEAD_SIZE), 1.0, 6.0, ((0, 16), (1, 8))),
        "completion_value_array": noise(key_of[2], (COMPLETION_COUNT * COMPLETION_SLOTS, KEY_VALUE_HEADS * HEAD_SIZE), 1.0, 6.0, ((0, 16), (1, 8))),
        "comp_dout": noise(key_of[3], (COMPLETION_COUNT * COMPLETION_SLOTS, QUERY_HEADS * HEAD_SIZE), 32.0, 192.0, ((0, 16), (1, 8))),
        "prompt_query_array": draw_prompt_query_array(jax.random.fold_in(key_of[11], 71), 0),
        "prompt_key_array": draw_prompt_key_array(jax.random.fold_in(key_of[11], 71), 0),
        "prompt_value_array": noise(key_of[6], (PROMPT_TOKENS, KEY_VALUE_HEADS * HEAD_SIZE), 1.0, 6.0, ((0, 16), (1, 8))),
        "prompt_output_cotangent": noise(key_of[7], (PROMPT_TOKENS, QUERY_HEADS * HEAD_SIZE), 8.0, 48.0, ((0, 16), (1, 8))),
        "lengths": uneven(key_of[8], COMPLETION_COUNT, 5 * COMPLETION_COUNT // 2, MAXB, 2).astype(jnp.int32),
        "slot_of": jax.random.permutation(key_of[9], COMPLETION_COUNT).astype(jnp.int32),
        "passes": draw_passes(jax.random.fold_in(key_of[11], 71), 0),
    }


MASKED = -1.0e30


def visible_mask(row_ids, key_ids, comp_rows, prompt_len, live_rows, prompt_base):
    is_comp = row_ids[:, None] < comp_rows
    key_prompt = key_ids[None, :] < prompt_len
    own_key = key_ids[None, :] - prompt_len
    comp_ok = key_prompt | ((own_key <= row_ids[:, None]) & (own_key < live_rows))
    prompt_pos = prompt_base + row_ids[:, None] - comp_rows
    prompt_ok = key_prompt & (key_ids[None, :] <= prompt_pos)
    return jnp.where(is_comp, comp_ok, prompt_ok)


def head_grads(queries, key_rows, value_rows, cotangent, visible, score_scale):
    query_f = queries.astype(jnp.float32)
    key_f = key_rows.astype(jnp.float32)
    value_f = value_rows.astype(jnp.float32)
    cot_f = cotangent.astype(jnp.float32)
    raw = jnp.einsum("rgd,kd->rgk", query_f, key_f) * score_scale
    scores = jnp.where(visible[:, None, :], raw, MASKED)
    row_top = jnp.max(scores, axis=2, keepdims=True)
    row_total = jnp.sum(jnp.exp(scores - row_top), axis=2, keepdims=True)
    weights = jnp.exp(scores - row_top) / row_total
    dweights = jnp.einsum("rgd,kd->rgk", cot_f, value_f)
    drift = jnp.sum(weights * dweights, axis=2, keepdims=True)
    dscores = lax.optimization_barrier((weights * (dweights - drift)).astype(jnp.bfloat16)).astype(jnp.float32)
    weights_b = lax.optimization_barrier(weights.astype(jnp.bfloat16)).astype(jnp.float32)
    query_grad = jnp.einsum("rgk,kd->rgd", dscores, key_f) * score_scale
    key_grad = jnp.einsum("rgk,rgd->kd", dscores, query_f) * score_scale
    value_grad = jnp.einsum("rgk,rgd->kd", weights_b, cot_f)
    return query_grad, key_grad, value_grad


def reference(completion_query_slots, completion_key_array, completion_value_array, comp_dout, prompt_query_array, prompt_key_array, prompt_value_array, prompt_output_cotangent, lengths, slot_of, passes):
    rewards = jnp.sum(passes, axis=1).astype(jnp.float32) / TESTS
    center = jnp.mean(rewards)
    advantage = rewards - center
    slots = jnp.arange(COMPLETION_COUNT, dtype=jnp.int32)
    blocks = jnp.sum(jnp.where(slot_of[:, None] == slots[None, :], lengths[:, None], 0), axis=0).astype(jnp.int32)
    live = (blocks * BLK).astype(jnp.int32)
    factor = advantage * MAXB / blocks.astype(jnp.float32)
    row_ids = jnp.arange(COMPLETION_SLOTS, dtype=jnp.int32)
    keep = (row_ids[None, :] < live[:, None]).astype(jnp.float32)
    dout_f = comp_dout.reshape(COMPLETION_COUNT, COMPLETION_SLOTS, QUERY_HEADS * HEAD_SIZE).astype(jnp.float32)
    completion_cotangent = (dout_f * factor[:, None, None] * keep[:, :, None]).astype(jnp.bfloat16)
    head_groups = QUERY_HEADS // KEY_VALUE_HEADS
    completion_query = completion_query_slots.reshape(COMPLETION_COUNT, COMPLETION_SLOTS, KEY_VALUE_HEADS, head_groups, HEAD_SIZE)
    completion_cotangents = completion_cotangent.reshape(COMPLETION_COUNT, COMPLETION_SLOTS, KEY_VALUE_HEADS, head_groups, HEAD_SIZE)
    completion_keys = completion_key_array.reshape(COMPLETION_COUNT, COMPLETION_SLOTS, KEY_VALUE_HEADS, HEAD_SIZE)
    completion_values = completion_value_array.reshape(COMPLETION_COUNT, COMPLETION_SLOTS, KEY_VALUE_HEADS, HEAD_SIZE)
    prompt_query_matrix = prompt_query_array.reshape(PROMPT_TOKENS, KEY_VALUE_HEADS, head_groups, HEAD_SIZE)
    prompt_cotangents = prompt_output_cotangent.reshape(PROMPT_TOKENS, KEY_VALUE_HEADS, head_groups, HEAD_SIZE)
    prompt_key_matrix = prompt_key_array.reshape(PROMPT_TOKENS, KEY_VALUE_HEADS, HEAD_SIZE)
    prompt_value_matrix = prompt_value_array.reshape(PROMPT_TOKENS, KEY_VALUE_HEADS, HEAD_SIZE)
    score_scale = HEAD_SIZE ** -0.5
    prompt_ids = jnp.arange(PROMPT_TOKENS, dtype=jnp.int32)
    prompt_visible = visible_mask(prompt_ids, prompt_ids, 0, PROMPT_TOKENS, 0, 0)
    all_ids = jnp.arange(PROMPT_TOKENS + COMPLETION_SLOTS, dtype=jnp.int32)

    def each_head_terms(kv_head):
        prompt_query_gradient, prompt_key_gradient, prompt_value_gradient = head_grads(prompt_query_matrix[:, kv_head], prompt_key_matrix[:, kv_head], prompt_value_matrix[:, kv_head], prompt_cotangents[:, kv_head], prompt_visible, score_scale)

        def per_slot(slot):
            key_rows = jnp.concatenate([prompt_key_matrix[:, kv_head], completion_keys[slot, :, kv_head]], axis=0)
            value_rows = jnp.concatenate([prompt_value_matrix[:, kv_head], completion_values[slot, :, kv_head]], axis=0)
            visible = visible_mask(row_ids, all_ids, COMPLETION_SLOTS, PROMPT_TOKENS, live[slot], 0)
            return head_grads(completion_query[slot, :, kv_head], key_rows, value_rows, completion_cotangents[slot, :, kv_head], visible, score_scale)

        completion_query_gradient, completion_key_gradient, completion_value_gradient = lax.map(per_slot, slots)
        prompt_key_grad = prompt_key_gradient + jnp.sum(completion_key_gradient[:, :PROMPT_TOKENS], axis=0)
        prompt_value_grad = prompt_value_gradient + jnp.sum(completion_value_gradient[:, :PROMPT_TOKENS], axis=0)
        return completion_query_gradient, completion_key_gradient[:, PROMPT_TOKENS:], completion_value_gradient[:, PROMPT_TOKENS:], prompt_query_gradient, prompt_key_grad, prompt_value_grad

    completion_query_gradient, completion_key_gradient, completion_value_gradient, prompt_query_gradient, prompt_key_gradient, prompt_value_gradient = lax.map(each_head_terms, jnp.arange(KEY_VALUE_HEADS, dtype=jnp.int32))
    comp_dq = jnp.transpose(completion_query_gradient, (1, 2, 0, 3, 4)).reshape(COMPLETION_COUNT * COMPLETION_SLOTS, QUERY_HEADS * HEAD_SIZE).astype(jnp.bfloat16)
    completion_key_gradients = jnp.transpose(completion_key_gradient, (1, 2, 0, 3)).reshape(COMPLETION_COUNT * COMPLETION_SLOTS, KEY_VALUE_HEADS * HEAD_SIZE).astype(jnp.bfloat16)
    completion_value_gradients = jnp.transpose(completion_value_gradient, (1, 2, 0, 3)).reshape(COMPLETION_COUNT * COMPLETION_SLOTS, KEY_VALUE_HEADS * HEAD_SIZE).astype(jnp.bfloat16)
    prompt_dq = jnp.transpose(prompt_query_gradient, (1, 0, 2, 3)).reshape(PROMPT_TOKENS, QUERY_HEADS * HEAD_SIZE).astype(jnp.bfloat16)
    prompt_key_gradients = jnp.transpose(prompt_key_gradient, (1, 0, 2)).reshape(PROMPT_TOKENS, KEY_VALUE_HEADS * HEAD_SIZE).astype(jnp.bfloat16)
    prompt_value_gradients = jnp.transpose(prompt_value_gradient, (1, 0, 2)).reshape(PROMPT_TOKENS, KEY_VALUE_HEADS * HEAD_SIZE).astype(jnp.bfloat16)
    return comp_dq, completion_key_gradients, completion_value_gradients, prompt_dq, prompt_key_gradients, prompt_value_gradients
```

```python
import functools
import jax
import jax.numpy as jnp
from jax import lax
from jax.experimental import pallas as pl
from jax.experimental.pallas import tpu as pltpu
from jax.sharding import PartitionSpec as P

MESH = pl.DeviceIdType.MESH
NG, NT, TESTS, MAXB, BLK = 16, 8, 32, 4, 128
F32, BF = jnp.float32, jnp.bfloat16
HEADS, D, CR, PR, PK = 8, 128, 512, 96, 1536
NB = CR // 128
NK = PK + CR
SCALE = D ** -0.5
C2 = SCALE * 1.4426950408889634

def dot(a, b, ca=1, cb=0):
    return lax.dot_general(a, b, (((ca,), (cb,)), ((), ())), preferred_element_type=F32)

def split(x):
    xs = x.astype(F32) * C2
    hi = xs.astype(BF)
    lo = (xs - hi.astype(F32)).astype(BF)
    return hi, lo

def compute_kernel(len_ref, slot_ref, rew, qc, dc, qp, dp, kv, kc, vc,
           dqc, dkc, dvc, dqp, part,
           kk, kkt, vt, W, DS, QT, OT, S0, S1, S2, S3, S4, T0, T1, T2, T3, T4, cot):
    S = [S0, S1, S2, S3, S4]
    T = [T0, T1, T2, T3, T4]
    g = lax.axis_index("group")
    blocks = jnp.int32(0)
    for c in range(NG):
        blocks = blocks + jnp.where(slot_ref[c] == g, len_ref[c], 0)
    live = blocks * BLK
    center = jnp.sum(rew[...], axis=0, keepdims=True) / NG
    adv = rew[pl.ds(g, 1), :] - center
    fac = adv * MAXB / jnp.broadcast_to(blocks.astype(F32), (1, D))
    kk[:PK] = kv[:, :D]
    kk[PK:] = kc[...]
    kt = jnp.transpose(kk[...])
    kkt[:D] = kt
    kkt[D:] = kt
    vt[:, :PK] = jnp.transpose(kv[:, D:])
    vt[:, PK:] = jnp.transpose(vc[...])
    row = lax.broadcasted_iota(jnp.int32, (CR, 1), 0)
    f = jnp.where(row < live, fac, 0.0)
    @pl.loop(0, HEADS)
    def _(h):
        c = pl.ds(pl.multiple_of(h * D, D), D)
        ct = (dc[:, c].astype(F32) * f).astype(BF)
        cot[:, c] = ct
        ctt = jnp.transpose(ct)
        qt = jnp.transpose(qc[:, c])
        for i in range(NB):
            cc = pl.ds(pl.multiple_of(i * 1024 + h * D, D), D)
            OT[:, cc] = ctt[:, i * 128:(i + 1) * 128]
            QT[:, cc] = qt[:, i * 128:(i + 1) * 128]
    OT[:, 4096:] = jnp.transpose(jnp.concatenate([dp[:, h * D:(h + 1) * D] for h in range(HEADS)], axis=0))
    QT[:, 4096:] = jnp.transpose(jnp.concatenate([qp[:, h * D:(h + 1) * D] for h in range(HEADS)], axis=0))
    for i in (0, 2):
        W[i * 1024:(i + 1) * 1024, PK + (i + 1) * 128:PK + (i + 2) * 128] = jnp.zeros((1024, 128), BF)
        DS[i * 1024:(i + 1) * 1024, PK + (i + 1) * 128:PK + (i + 2) * 128] = jnp.zeros((1024, 128), BF)

    nks = [PK + 128 * (i + 1) for i in range(NB)] + [PK]

    def mm1(t, h):
        c = pl.ds(pl.multiple_of(h * D, D), D)
        if t < NB:
            q = qc[t * 128:(t + 1) * 128, c]
            o = cot[t * 128:(t + 1) * 128, c]
        else:
            q = qp[:, c]
            o = dp[:, c]
        hi, lo = split(q)
        S[t][...] = dot(jnp.concatenate([hi, lo], axis=1), kkt[:, :nks[t]])
        T[t][...] = dot(o, vt[:, :nks[t]])

    def soft(t, h):
        s = S[t][...]
        n = nks[t]
        if t < NB:
            r = lax.broadcasted_iota(jnp.int32, (128, 128), 0)
            k = lax.broadcasted_iota(jnp.int32, (128, 128), 1)
            s = jnp.concatenate([s[:, :n - 128], jnp.where(k <= r, s[:, n - 128:], -1e30)], axis=1)
        else:
            r = lax.broadcasted_iota(jnp.int32, (PR, n), 0) + g * PR
            k = lax.broadcasted_iota(jnp.int32, (PR, n), 1)
            s = jnp.where(k <= r, s, -1e30)
        m = jnp.max(s, axis=1, keepdims=True)
        e = jnp.exp2(s - m)
        tot = jnp.sum(e, axis=1, keepdims=True)
        w = e * (1.0 / tot)
        d = T[t][...]
        drift = jnp.sum(w * d, axis=1, keepdims=True)
        ds = (w * (d - drift)).astype(BF)
        if t < NB:
            rr = pl.ds(pl.multiple_of(t * 1024 + h * 128, 128), 128)
        else:
            rr = pl.ds(pl.multiple_of(4096 + h * PR, 32), PR)
        W[rr, :n] = w.astype(BF)
        DS[rr, :n] = ds
        return ds

    def mm2(t, h):
        c = pl.ds(pl.multiple_of(h * D, D), D)
        n = nks[t]
        if t < NB:
            rr = pl.ds(pl.multiple_of(t * 1024 + h * 128, 128), 128)
            dqc[t * 128:(t + 1) * 128, c] = (dot(DS[rr, :n], kk[:n]) * SCALE).astype(BF)
        else:
            rr = pl.ds(pl.multiple_of(4096 + h * PR, 32), PR)
            dqp[:, c] = (dot(DS[rr, :n], kk[:n]) * SCALE).astype(BF)

    mm1(0, 0)
    @pl.loop(0, HEADS)
    def _(h):
        for t in range(5):
            if t < 4:
                mm1(t + 1, h)
            else:
                mm1(0, lax.rem(h + 1, HEADS))
            soft(t, h)
            mm2(t, h)
    for b in range(NK // 256):
        lo, hi = b * 256, (b + 1) * 256
        if lo < PK:
            r0, r1 = 0, 4096 + HEADS * PR
        else:
            r0, r1 = ((lo - PK) // 128) * 1024, 4096
        gv = jnp.transpose(dot(OT[:, r0:r1], W[r0:r1, lo:hi])).astype(BF)
        gk = jnp.transpose(dot(QT[:, r0:r1], DS[r0:r1, lo:hi]) * SCALE).astype(BF)
        if lo < PK:
            part[lo:hi, :D] = gk
            part[lo:hi, D:] = gv
        else:
            dkc[lo - PK:hi - PK] = gk
            dvc[lo - PK:hi - PK] = gv

def compute(lengths, slot_of, rew, qc, dc, qp, dp, kv, kc, vc):
    v = pl.BlockSpec(memory_space=pltpu.VMEM)
    sm = pl.BlockSpec(memory_space=pltpu.SMEM)
    R = 4096 + HEADS * PR
    nks = [PK + 128 * (i + 1) for i in range(NB)] + [PK]
    rows = [128] * 4 + [PR]
    return pl.pallas_call(
        compute_kernel,
        out_shape=(jax.ShapeDtypeStruct((CR, 1024), BF), jax.ShapeDtypeStruct((CR, D), BF), jax.ShapeDtypeStruct((CR, D), BF),
                   jax.ShapeDtypeStruct((PR, 1024), BF), jax.ShapeDtypeStruct((PK, 2 * D), BF)),
        in_specs=[sm, sm] + [v] * 8, out_specs=[v] * 5,
        scratch_shapes=[pltpu.VMEM((NK, D), BF), pltpu.VMEM((2 * D, NK), BF), pltpu.VMEM((D, NK), BF),
                        pltpu.VMEM((R, NK), BF), pltpu.VMEM((R, NK), BF), pltpu.VMEM((D, R), BF), pltpu.VMEM((D, R), BF)]
                       + [pltpu.VMEM((r, n), F32) for r, n in zip(rows, nks)] * 2 + [pltpu.VMEM((CR, 1024), BF)],
        compiler_params=pltpu.CompilerParams(vmem_limit_bytes=63 << 20),
        name="attention_backward",
    )(lengths, slot_of, rew, qc, dc, qp, dp, kv, kc, vc)


def peers(g, t):
    chip, core = g // 2, lax.rem(g, 2)
    same = [(2 * lax.rem(chip + j, 8) + core, t) for j in range(1, 8)]
    sib = (2 * chip + 1 - core, t)
    return chip, core, same, sib


def gather_kernel(pk, pv, passes, kv, rew, own, cnt, cnt_in, rew_in, ss, rs, cs, cr, ws, wr):
    g, t = lax.axis_index("group"), lax.axis_index("tensor")
    chip, core, same, sib = peers(g, t)
    group = [(lax.rem(g + j, NG), t) for j in range(1, NG)]
    tens = [(g, lax.rem(t + j, NT)) for j in range(1, NT)]
    barrier = pltpu.get_barrier_semaphore()
    for d in group + tens:
        pl.semaphore_signal(barrier, inc=1, device_id=d, device_id_type=MESH)
    own[:, :D] = pk[...]
    own[:, D:] = pv[...]
    cnt[...] = jnp.broadcast_to(jnp.sum(passes[...].astype(F32), axis=1, keepdims=True), (8, D))
    pl.semaphore_wait(barrier, len(group) + len(tens))
    mine = pl.ds(pl.multiple_of(g * PR, 32), PR)

    def rc(src, dst, s, r, d):
        return pltpu.make_async_remote_copy(src_ref=src, dst_ref=dst, send_sem=s, recv_sem=r, device_id=d, device_id_type=MESH)

    c1 = [rc(cnt, cnt_in.at[j], cs.at[j], cr.at[j], tens[j]) for j in range(NT - 1)]
    for c in c1:
        c.start()
    out = [rc(own, kv.at[mine], ss.at[j], rs.at[j], same[j - 1] if j else sib) for j in range(8)]
    for c in out:
        c.start()
    kv[mine, :] = own[...]
    for c in c1:
        c.wait_recv()
    total = cnt[...]
    for j in range(NT - 1):
        total = total + cnt_in[j]
    r8 = total / TESTS
    rew_in[pl.ds(g, 1)] = r8[None]
    c2 = [rc(rew_in.at[pl.ds(g, 1)], rew_in.at[pl.ds(g, 1)], ws.at[j], wr.at[j], group[j]) for j in range(NG - 1)]
    for c in c2:
        c.start()
    fwd = []
    for j in range(1, 8):
        out[j].wait_recv()
        src = 2 * lax.rem(chip - j + 8, 8) + core
        rows = pl.ds(pl.multiple_of(src * PR, 32), PR)
        f = rc(kv.at[rows], kv.at[rows], ss.at[7 + j], rs.at[7 + j], sib)
        f.start()
        fwd.append(f)
    for c in c2:
        c.wait_recv()
    for s in range(NG):
        rew[s:s + 1, :] = rew_in[s][:1]
    out[0].wait_recv()
    for f in fwd:
        f.wait_recv()
    for c in c1 + out + c2 + fwd:
        c.wait_send()


def gather(pk, pv, passes):
    v = pl.BlockSpec(memory_space=pltpu.VMEM)
    dma = pltpu.SemaphoreType.DMA
    return pl.pallas_call(
        gather_kernel,
        out_shape=(jax.ShapeDtypeStruct((PK, 2 * D), BF), jax.ShapeDtypeStruct((NG, D), F32)),
        in_specs=[v] * 3, out_specs=[v] * 2,
        scratch_shapes=[pltpu.VMEM((PR, 2 * D), BF), pltpu.VMEM((8, D), F32), pltpu.VMEM((NT - 1, 8, D), F32), pltpu.VMEM((NG, 8, D), F32),
                        dma((15,)), dma((15,)), dma((NT - 1,)), dma((NT - 1,)), dma((NG - 1,)), dma((NG - 1,))],
        compiler_params=pltpu.CompilerParams(collective_id=1, has_side_effects=True),
        name="gather_prompt",
    )(pk, pv, passes)


def scatter_kernel(part, dk, dv, inc, summed, got, s1, r1, s2, r2):
    g, t = lax.axis_index("group"), lax.axis_index("tensor")
    chip, core, same, sib = peers(g, t)
    barrier = pltpu.get_barrier_semaphore()
    for d in same + [sib]:
        pl.semaphore_signal(barrier, inc=1, device_id=d, device_id_type=MESH)
    pl.semaphore_wait(barrier, 8)

    def rows(c, k):
        return pl.ds(pl.multiple_of((2 * c + k) * PR, 32), PR)

    def rc(src, dst, s, r, d):
        return pltpu.make_async_remote_copy(src_ref=src, dst_ref=dst, send_sem=s, recv_sem=r, device_id=d, device_id_type=MESH)

    order = [1, 2, 3, 4, 5, 6, 7, 0]
    chips = [lax.rem(chip + j, 8) for j in order]
    first = [rc(part.at[rows(chips[i], 1 - core)], inc.at[i], s1.at[i], r1.at[i], sib) for i in range(8)]
    for c in first:
        c.start()
    second = []
    for i in range(8):
        first[i].wait_recv()
        x = inc[i].astype(F32) + part[rows(chips[i], core), :].astype(F32)
        if i < 7:
            summed[i] = x.astype(BF)
            c = rc(summed.at[i], got.at[i], s2.at[i], r2.at[i], same[i])
            c.start()
            second.append(c)
        else:
            total = x
    for i in range(7):
        second[i].wait_recv()
        total = total + got[i].astype(F32)
    dk[...] = total[:, :D].astype(BF)
    dv[...] = total[:, D:].astype(BF)
    for c in first + second:
        c.wait_send()


def scatter(part):
    v = pl.BlockSpec(memory_space=pltpu.VMEM)
    dma = pltpu.SemaphoreType.DMA
    return pl.pallas_call(
        scatter_kernel,
        out_shape=(jax.ShapeDtypeStruct((PR, D), BF), jax.ShapeDtypeStruct((PR, D), BF)),
        in_specs=[v], out_specs=[v] * 2,
        scratch_shapes=[pltpu.VMEM((8, PR, 2 * D), BF), pltpu.VMEM((7, PR, 2 * D), BF), pltpu.VMEM((7, PR, 2 * D), BF),
                        dma((8,)), dma((8,)), dma((7,)), dma((7,))],
        compiler_params=pltpu.CompilerParams(collective_id=2, has_side_effects=True),
        name="scatter_prompt",
    )(part)


def per_device(qc, kc, vc, dc, qp, pk, pv, dp, lengths, slot_of, passes):
    kv, rew = gather(pk, pv, passes)
    dqc, dkc, dvc, dqp, part = compute(lengths, slot_of, rew, qc, dc, qp, dp, kv, kc, vc)
    dk, dv = scatter(part)
    return dqc, dkc, dvc, dqp, dk, dv


def solution(mesh):
    gt = P("group", "tensor")
    return jax.shard_map(per_device, mesh=mesh, in_specs=(gt,) * 8 + (P(), P(), gt), out_specs=(gt,) * 6, check_vma=False)
```

```python
import jax
import jax.numpy as jnp
from jax import lax
from jax.experimental import pallas as pl
from jax.experimental.pallas import tpu as pltpu
from jax.sharding import PartitionSpec as P

MESH = pl.DeviceIdType.MESH
NG, NT, TESTS, MAXB, BLK = 16, 8, 32, 4, 128
F32, BF = jnp.float32, jnp.bfloat16
HEADS, D, CR, PR, PK = 8, 128, 512, 96, 1536
NB = CR // 128
NK = PK + CR
RC = HEADS * CR
RA = RC + HEADS * PR
SCALE = D ** -0.5
C2 = SCALE * 1.4426950408889634
NKS = [PK + 128 * (i + 1) for i in range(NB)] + [PK]
ROWS = [128] * NB + [PR]
CHIPS = NG // 2


def dot(a, b):
    return lax.dot_general(a, b, (((1,), (0,)), ((), ())), preferred_element_type=F32)


def backward_kernel(qc_h, kc_h, vc_h, dc_h, qp_h, pk_h, pv_h, dp_h, len_h, slot_h, passes_h,
                    dqc_h, dkc_h, dvc_h, dqp_h, dk_h, dv_h,
                    qc, dc, qp, dp, lens, slots, passes, kv, kc, vc, kk, kkt, vt, W, DS, QT, OT, RF, QP, OP,
                    dqc, dqp, dkc, dvc, dk, dv, part, inc, summed, got, cnt, cnt_in, rew,
                    S0, S1, S2, S3, S4, T0, T1, T2, T3, T4,
                    ls, os, gs, gr, cs, cr, ws, wr, s1, r1, s2, r2):
    S, T = [S0, S1, S2, S3, S4], [T0, T1, T2, T3, T4]
    g, t_ax = lax.axis_index("group"), lax.axis_index("tensor")
    chip, core = g // 2, lax.rem(g, 2)
    same = [(2 * lax.rem(chip + j, CHIPS) + core, t_ax) for j in range(1, CHIPS)]
    sib = (2 * chip + 1 - core, t_ax)
    group = [(lax.rem(g + j, NG), t_ax) for j in range(1, NG)]
    tens = [(g, lax.rem(t_ax + j, NT)) for j in range(1, NT)]

    def rc(src, dst, s, r, d):
        return pltpu.make_async_remote_copy(src_ref=src, dst_ref=dst, send_sem=s, recv_sem=r, device_id=d, device_id_type=MESH)

    def shard(s):
        return pl.ds(pl.multiple_of(s * PR, 32), PR)

    barrier = pltpu.get_barrier_semaphore()
    for d in group + tens:
        pl.semaphore_signal(barrier, inc=1, device_id=d, device_id_type=MESH)
    mine = shard(g)
    loads = [pltpu.make_async_copy(a, b, ls.at[i]) for i, (a, b) in enumerate([
        (pk_h, kv.at[mine, pl.ds(0, D)]), (pv_h, kv.at[mine, pl.ds(D, D)]), (passes_h, passes), (kc_h, kc), (vc_h, vc),
        (len_h, lens), (slot_h, slots), (qc_h, qc), (dc_h, dc), (qp_h, qp), (dp_h, dp)])]
    for c in loads:
        c.start()
    for i in range(0, NB, 2):
        z = jnp.zeros((1024, 128), BF)
        W[i * 1024:(i + 1) * 1024, PK + (i + 1) * 128:PK + (i + 2) * 128] = z
        DS[i * 1024:(i + 1) * 1024, PK + (i + 1) * 128:PK + (i + 2) * 128] = z
    for c in loads:
        c.wait()
    cnt[...] = jnp.broadcast_to(jnp.sum(passes[...].astype(F32), axis=1, keepdims=True), (8, D))
    kk[PK:] = kc[...]
    kt = jnp.transpose(kc[...])
    kkt[:D, PK:] = kt
    kkt[D:, PK:] = kt
    vt[:, PK:] = jnp.transpose(vc[...])
    pl.semaphore_wait(barrier, len(group) + len(tens))

    c1 = [rc(cnt, cnt_in.at[j], cs.at[j], cr.at[j], tens[j]) for j in range(NT - 1)]
    out = [rc(kv.at[mine], kv.at[mine], gs.at[j], gr.at[j], same[j - 1] if j else sib) for j in range(CHIPS)]
    for c in c1 + out:
        c.start()
    for c in c1:
        c.wait_recv()
    total = cnt[...]
    for j in range(NT - 1):
        total = total + cnt_in[j]
    rew[pl.ds(g, 1)] = (total / TESTS)[None]
    c2 = [rc(rew.at[pl.ds(g, 1)], rew.at[pl.ds(g, 1)], ws.at[j], wr.at[j], group[j]) for j in range(NG - 1)]
    for c in c2:
        c.start()
    fwd = []
    for j in range(1, CHIPS):
        out[j].wait_recv()
        rows = shard(2 * lax.rem(chip - j + CHIPS, CHIPS) + core)
        f = rc(kv.at[rows], kv.at[rows], gs.at[CHIPS - 1 + j], gr.at[CHIPS - 1 + j], sib)
        f.start()
        fwd.append(f)
    out[0].wait_recv()
    for f in fwd:
        f.wait_recv()
    kp = kv[:, :D]
    kk[:PK] = kp
    kt = jnp.transpose(kp)
    kkt[:D, :PK] = kt
    kkt[D:, :PK] = kt
    vt[:, :PK] = jnp.transpose(kv[:, D:])

    def cols(h):
        return pl.ds(pl.multiple_of(h * D, D), D)

    def rows_of(t, h):
        if t < NB:
            return pl.multiple_of(t * 1024 + h * 128, 128)
        return pl.multiple_of(RC + h * PR, 32)

    def qo(t, h):
        c = cols(h)
        if t < NB:
            return qc[t * 128:(t + 1) * 128, c], dc[t * 128:(t + 1) * 128, c]
        return qp[:, c], dp[:, c]

    def products(t, h):
        q, o = qo(t, h)
        n = NKS[t]
        xs = q.astype(F32) * C2
        hi = xs.astype(BF)
        lo = (xs - hi.astype(F32)).astype(BF)
        s = dot(jnp.concatenate([hi, lo], axis=1), kkt[:, :n])
        if t < NB:
            r = lax.broadcasted_iota(jnp.int32, (128, 128), 0)
            k = lax.broadcasted_iota(jnp.int32, (128, 128), 1)
            s = jnp.concatenate([s[:, :n - 128], jnp.where(k <= r, s[:, n - 128:], -1e30)], axis=1)
        else:
            r = lax.broadcasted_iota(jnp.int32, s.shape, 0) + g * PR
            k = lax.broadcasted_iota(jnp.int32, s.shape, 1)
            s = jnp.where(k <= r, s, -1e30)
        S[t][...] = s
        T[t][...] = dot(o, vt[:, :n])

    products(0, 0)
    for c in c2:
        c.wait_recv()
    center = rew[0]
    for s in range(1, NG):
        center = center + rew[s]
    blocks = jnp.sum(jnp.where(slots[...] == g, lens[...], 0).astype(F32), axis=1, keepdims=True)
    adv = rew[pl.ds(g, 1)][0][:1] - (center / NG)[:1]
    fac = adv * MAXB / blocks
    live = blocks * BLK

    def softmax(t, h):
        n = NKS[t]
        rr = rows_of(t, h)
        s = S[t][...]
        m = jnp.max(s, axis=1, keepdims=True)
        e = jnp.exp2(s - m)
        tot = jnp.sum(e, axis=1, keepdims=True)
        d = T[t][...]
        r = 1.0 / tot
        drift = jnp.sum(e * d, axis=1, keepdims=True) * r
        out = pl.ds(rr, ROWS[t])
        W[out, :n] = e.astype(BF)
        DS[out, :n] = (e * (d - drift)).astype(BF)
        if t < NB:
            row = lax.broadcasted_iota(jnp.int32, (128, D), 0) + t * 128
            r = r * jnp.where(row.astype(F32) < live, fac, 0.0)
        else:
            r = jnp.broadcast_to(r, (PR, D))
        RF[out, :] = r * SCALE
        q, o = qo(t, h)
        qs = (q.astype(F32) * (r * SCALE)).astype(BF)
        os_ = (o.astype(F32) * r).astype(BF)
        if t < NB:
            c = pl.ds(rr, 128)
            QT[:, c] = jnp.transpose(qs)
            OT[:, c] = jnp.transpose(os_)
        else:
            c = pl.ds(rr - RC, PR)
            QP[c, :] = qs
            OP[c, :] = os_

    @pl.loop(0, HEADS)
    def _(h):
        for t in range(5):
            if t < 4:
                products(t + 1, h)
            else:
                products(0, lax.rem(h + 1, HEADS))
            softmax(t, h)
    QT[:, RC:] = jnp.transpose(QP[...])
    OT[:, RC:] = jnp.transpose(OP[...])

    def key_block(b):
        lo, hi = b * 256, (b + 1) * 256
        r0, r1_ = (0, RA) if lo < PK else (((lo - PK) // 128) * 1024, RC)
        gv = jnp.transpose(dot(OT[:, r0:r1_], W[r0:r1_, lo:hi])).astype(BF)
        gk = jnp.transpose(dot(QT[:, r0:r1_], DS[r0:r1_, lo:hi])).astype(BF)
        if lo < PK:
            part[lo:hi, :D] = gk
            part[lo:hi, D:] = gv
        else:
            dkc[lo - PK:hi - PK] = gk
            dvc[lo - PK:hi - PK] = gv

    first = [rc(part.at[shard(2 * c + 1 - core)], inc.at[c], s1.at[c], r1.at[c], sib) for c in range(CHIPS)]
    second = [rc(summed.at[c], got.at[chip], s2.at[c], r2.at[chip], (2 * c + core, t_ax)) for c in range(CHIPS)]

    def pass_on(c):
        first[c].wait_recv()
        x = inc[c].astype(F32) + part[shard(2 * c + core), :].astype(F32)
        summed[c] = x.astype(BF)
        pl.when(chip != c)(second[c].start)

    started = 0
    for b in range(PK // 256):
        key_block(b)
        ready = ((b + 1) * 256 // PR) // 2
        for c in range(started, ready):
            first[c].start()
        if b:
            for c in range(passed, started):
                pass_on(c)
        passed, started = started, ready
    for b in range(PK // 256, NK // 256):
        key_block(b)
    for c in range(passed, CHIPS):
        pass_on(c)

    stores = [pltpu.make_async_copy(a, b, os.at[i]) for i, (a, b) in enumerate([
        (dkc, dkc_h), (dvc, dvc_h), (dqp, dqp_h), (dk, dk_h), (dv, dv_h)])]
    stores += [pltpu.make_async_copy(dqc.at[pl.ds(t * 128, 128)], dqc_h.at[pl.ds(t * 128, 128)], os.at[5 + t]) for t in range(NB)]
    stores[0].start()
    stores[1].start()
    for t in range(5):
        n, rws = NKS[t], ROWS[t]
        r0 = t * 1024 if t < NB else RC
        for h in range(0, HEADS, 2):
            a, b = r0 + h * rws, r0 + (h + 2) * rws
            x = dot(DS[a:b, :n], kk[:n]) * RF[a:b, :]
            for j in range(2):
                y = x[j * rws:(j + 1) * rws].astype(BF)
                if t < NB:
                    dqc[t * 128:(t + 1) * 128, (h + j) * D:(h + j + 1) * D] = y
                else:
                    dqp[:, (h + j) * D:(h + j + 1) * D] = y
        stores[5 + t if t < NB else 2].start()

    tot = inc[pl.ds(chip, 1)][0].astype(F32) + part[shard(g), :].astype(F32)
    for j in range(1, CHIPS):
        s = lax.rem(chip + j, CHIPS)
        rc(summed.at[0], got.at[s], s2.at[0], r2.at[s], same[0]).wait_recv()
        tot = tot + got[pl.ds(s, 1)][0].astype(F32)
    dk[...] = tot[:, :D].astype(BF)
    dv[...] = tot[:, D:].astype(BF)
    stores[3].start()
    stores[4].start()
    for c in c1 + c2 + out + fwd + first:
        c.wait_send()
    for c in range(CHIPS):
        pl.when(chip != c)(second[c].wait_send)
    for c in stores:
        c.wait()


def backward(qc, kc, vc, dc, qp, pk, pv, dp, lengths, slot_of, passes):
    hbm = pl.BlockSpec(memory_space=pltpu.HBM)
    dma = lambda n: pltpu.SemaphoreType.DMA((n,))
    b = lambda *s: pltpu.VMEM(s, BF)
    f = lambda *s: pltpu.VMEM(s, F32)
    i = lambda *s: pltpu.VMEM(s, jnp.int32)
    o = lambda *s: jax.ShapeDtypeStruct(s, BF)
    return pl.pallas_call(
        backward_kernel,
        out_shape=(o(CR, 1024), o(CR, D), o(CR, D), o(PR, 1024), o(PR, D), o(PR, D)),
        in_specs=[hbm] * 11, out_specs=[hbm] * 6,
        scratch_shapes=[b(CR, 1024), b(CR, 1024), b(PR, 1024), b(PR, 1024), i(1, 16), i(1, 16), i(1, 4),
                        b(PK, 2 * D), b(CR, D), b(CR, D), b(NK, D), b(2 * D, NK), b(D, NK), b(RA, NK), b(RA, NK), b(D, RA), b(D, RA),
                        f(RA, D), b(HEADS * PR, D), b(HEADS * PR, D),
                        b(CR, 1024), b(PR, 1024), b(CR, D), b(CR, D), b(PR, D), b(PR, D), b(PK, 2 * D),
                        b(CHIPS, PR, 2 * D), b(CHIPS, PR, 2 * D), b(CHIPS, PR, 2 * D), f(8, D), f(NT - 1, 8, D), f(NG, 8, D)]
                       + [f(r, n) for r, n in zip(ROWS, NKS)] * 2
                       + [dma(11), dma(9), dma(2 * CHIPS - 1), dma(2 * CHIPS - 1), dma(NT - 1), dma(NT - 1), dma(NG - 1), dma(NG - 1),
                          dma(CHIPS), dma(CHIPS), dma(CHIPS), dma(CHIPS)],
        compiler_params=pltpu.CompilerParams(collective_id=1, has_side_effects=True, vmem_limit_bytes=63 << 20),
        name="attention_backward",
    )(qc, kc, vc, dc, qp, pk, pv, dp, lengths.reshape(1, 16), slot_of.reshape(1, 16), passes)


def result_kernel(*refs):
    n = (len(refs) - 1) // 2
    cs = [pltpu.make_async_copy(refs[i], refs[n + i], refs[-1].at[i]) for i in range(n)]
    for c in cs:
        c.start()
    for c in cs:
        c.wait()


def results(*xs):
    hbm = pl.BlockSpec(memory_space=pltpu.HBM)
    return pl.pallas_call(
        result_kernel, out_shape=tuple(jax.ShapeDtypeStruct(x.shape, x.dtype) for x in xs),
        in_specs=[hbm] * len(xs), out_specs=[hbm] * len(xs),
        scratch_shapes=[pltpu.SemaphoreType.DMA((len(xs),))], name="write_results",
    )(*xs)


def per_device(*args):
    return results(*backward(*args))


def solution(mesh):
    gt = P("group", "tensor")
    return jax.shard_map(per_device, mesh=mesh, in_specs=(gt,) * 8 + (P(), P(), gt), out_specs=(gt,) * 6, check_vma=False)
```

```python
import jax
import jax.numpy as jnp
from jax import lax
from jax.experimental import pallas as pl
from jax.experimental.pallas import tpu as pltpu
from jax.sharding import PartitionSpec as P

MESH = pl.DeviceIdType.MESH
NG, NT, TESTS, MAXB, BLK = 16, 8, 32, 4, 128
F32, BF = jnp.float32, jnp.bfloat16
HEADS, D, CR, PR, PK = 8, 128, 512, 96, 1536
NB = CR // 128
NK = PK + CR
RC = HEADS * CR
RA = RC + HEADS * PR
SCALE = D ** -0.5
C2 = SCALE * 1.4426950408889634
NKS = [PK + 128 * (i + 1) for i in range(NB)] + [PK]
ROWS = [128] * NB + [PR]
CHIPS = NG // 2


def dot(a, b):
    return lax.dot_general(a, b, (((1,), (0,)), ((), ())), preferred_element_type=F32)


def backward_kernel(qc_h, kc_h, vc_h, dc_h, qp_h, pk_h, pv_h, dp_h, len_h, slot_h, passes_h,
                    dqc_h, dkc_h, dvc_h, dqp_h, dk_h, dv_h,
                    qc, dc, qp, dp, lens, slots, passes, kv, kc, vc, kk, kkt, vt, W, DS, QT, OT, RF, QP, OP,
                    dqc, dqp, dkc, dvc, dk, dv, part, inc, summed, got, cnt, cnt_in, rew,
                    S0, S1, S2, S3, S4, T0, T1, T2, T3, T4,
                    ls, os, gs, gr, cs, cr, ws, wr, s1, r1, s2, r2):
    S, T = [S0, S1, S2, S3, S4], [T0, T1, T2, T3, T4]
    g, t_ax = lax.axis_index("group"), lax.axis_index("tensor")
    chip, core = g // 2, lax.rem(g, 2)
    same = [(2 * lax.rem(chip + j, CHIPS) + core, t_ax) for j in range(1, CHIPS)]
    sib = (2 * chip + 1 - core, t_ax)
    group = [(lax.rem(g + j, NG), t_ax) for j in range(1, NG)]
    tens = [(g, lax.rem(t_ax + j, NT)) for j in range(1, NT)]

    def rc(src, dst, s, r, d):
        return pltpu.make_async_remote_copy(src_ref=src, dst_ref=dst, send_sem=s, recv_sem=r, device_id=d, device_id_type=MESH)

    def shard(s):
        return pl.ds(pl.multiple_of(s * PR, 32), PR)

    barrier = pltpu.get_barrier_semaphore()
    for d in group + tens:
        pl.semaphore_signal(barrier, inc=1, device_id=d, device_id_type=MESH)
    mine = shard(g)
    loads = [pltpu.make_async_copy(a, b, ls.at[i]) for i, (a, b) in enumerate([
        (pk_h, kv.at[mine, pl.ds(0, D)]), (pv_h, kv.at[mine, pl.ds(D, D)]), (passes_h, passes), (kc_h, kc), (vc_h, vc),
        (len_h, lens), (slot_h, slots), (qc_h, qc), (dc_h, dc), (qp_h, qp), (dp_h, dp)])]
    for c in loads:
        c.start()
    for i in range(0, NB, 2):
        z = jnp.zeros((1024, 128), BF)
        W[i * 1024:(i + 1) * 1024, PK + (i + 1) * 128:PK + (i + 2) * 128] = z
        DS[i * 1024:(i + 1) * 1024, PK + (i + 1) * 128:PK + (i + 2) * 128] = z
    for c in loads:
        c.wait()
    cnt[...] = jnp.broadcast_to(jnp.sum(passes[...].astype(F32), axis=1, keepdims=True), (8, D))
    kk[PK:] = kc[...]
    kt = jnp.transpose(kc[...])
    kkt[:D, PK:] = kt
    kkt[D:, PK:] = kt
    vt[:, PK:] = jnp.transpose(vc[...])
    pl.semaphore_wait(barrier, len(group) + len(tens))

    c1 = [rc(cnt, cnt_in.at[j], cs.at[j], cr.at[j], tens[j]) for j in range(NT - 1)]
    out = [rc(kv.at[mine], kv.at[mine], gs.at[j], gr.at[j], same[j - 1] if j else sib) for j in range(CHIPS)]
    for c in c1 + out:
        c.start()
    for c in c1:
        c.wait_recv()
    total = cnt[...]
    for j in range(NT - 1):
        total = total + cnt_in[j]
    rew[pl.ds(g, 1)] = (total / TESTS)[None]
    c2 = [rc(rew.at[pl.ds(g, 1)], rew.at[pl.ds(g, 1)], ws.at[j], wr.at[j], group[j]) for j in range(NG - 1)]
    for c in c2:
        c.start()
    fwd = []
    for j in range(1, CHIPS):
        out[j].wait_recv()
        rows = shard(2 * lax.rem(chip - j + CHIPS, CHIPS) + core)
        f = rc(kv.at[rows], kv.at[rows], gs.at[CHIPS - 1 + j], gr.at[CHIPS - 1 + j], sib)
        f.start()
        fwd.append(f)
    out[0].wait_recv()
    for f in fwd:
        f.wait_recv()
    kp = kv[:, :D]
    kk[:PK] = kp
    kt = jnp.transpose(kp)
    kkt[:D, :PK] = kt
    kkt[D:, :PK] = kt
    vt[:, :PK] = jnp.transpose(kv[:, D:])

    def cols(h):
        return pl.ds(pl.multiple_of(h * D, D), D)

    def rows_of(t, h):
        if t < NB:
            return pl.multiple_of(t * 1024 + h * 128, 128)
        return pl.multiple_of(RC + h * PR, 32)

    def qo(t, h):
        c = cols(h)
        if t < NB:
            return qc[t * 128:(t + 1) * 128, c], dc[t * 128:(t + 1) * 128, c]
        return qp[:, c], dp[:, c]

    def products(t, h):
        q, o = qo(t, h)
        n = NKS[t]
        xs = q.astype(F32) * C2
        hi = xs.astype(BF)
        lo = (xs - hi.astype(F32)).astype(BF)
        s = dot(jnp.concatenate([hi, lo], axis=1), kkt[:, :n])
        if t < NB:
            r = lax.broadcasted_iota(jnp.int32, (128, 128), 0)
            k = lax.broadcasted_iota(jnp.int32, (128, 128), 1)
            s = jnp.concatenate([s[:, :n - 128], jnp.where(k <= r, s[:, n - 128:], -1e30)], axis=1)
        else:
            r = lax.broadcasted_iota(jnp.int32, s.shape, 0) + g * PR
            k = lax.broadcasted_iota(jnp.int32, s.shape, 1)
            s = jnp.where(k <= r, s, -1e30)
        S[t][...] = s
        T[t][...] = dot(o, vt[:, :n])

    products(0, 0)
    for c in c2:
        c.wait_recv()
    center = rew[0]
    for s in range(1, NG):
        center = center + rew[s]
    blocks = jnp.sum(jnp.where(slots[...] == g, lens[...], 0).astype(F32), axis=1, keepdims=True)
    adv = rew[pl.ds(g, 1)][0][:1] - (center / NG)[:1]
    fac = adv * MAXB / blocks
    live = blocks * BLK

    def softmax(t, h):
        n = NKS[t]
        rr = rows_of(t, h)
        s = S[t][...]
        m = jnp.max(s, axis=1, keepdims=True)
        e = jnp.exp2(s - m)
        tot = jnp.sum(e, axis=1, keepdims=True)
        d = T[t][...]
        r = 1.0 / tot
        drift = jnp.sum(e * d, axis=1, keepdims=True) * r
        out = pl.ds(rr, ROWS[t])
        W[out, :n] = e.astype(BF)
        DS[out, :n] = (e * (d - drift)).astype(BF)
        if t < NB:
            row = lax.broadcasted_iota(jnp.int32, (128, D), 0) + t * 128
            r = r * jnp.where(row.astype(F32) < live, fac, 0.0)
        else:
            r = jnp.broadcast_to(r, (PR, D))
        RF[out, :] = r * SCALE
        q, o = qo(t, h)
        qs = (q.astype(F32) * (r * SCALE)).astype(BF)
        os_ = (o.astype(F32) * r).astype(BF)
        if t < NB:
            c = pl.ds(rr, 128)
            QT[:, c] = jnp.transpose(qs)
            OT[:, c] = jnp.transpose(os_)
        else:
            c = pl.ds(rr - RC, PR)
            QP[c, :] = qs
            OP[c, :] = os_

    @pl.loop(0, HEADS)
    def _(h):
        for t in range(5):
            if t < 4:
                products(t + 1, h)
            else:
                products(0, lax.rem(h + 1, HEADS))
            softmax(t, h)
    QT[:, RC:] = jnp.transpose(QP[...])
    OT[:, RC:] = jnp.transpose(OP[...])

    def key_block(b):
        lo, hi = b * 256, (b + 1) * 256
        r0, r1_ = (0, RA) if lo < PK else (((lo - PK) // 128) * 1024, RC)
        gv = jnp.transpose(dot(OT[:, r0:r1_], W[r0:r1_, lo:hi])).astype(BF)
        gk = jnp.transpose(dot(QT[:, r0:r1_], DS[r0:r1_, lo:hi])).astype(BF)
        if lo < PK:
            part[lo:hi, :D] = gk
            part[lo:hi, D:] = gv
        else:
            dkc[lo - PK:hi - PK] = gk
            dvc[lo - PK:hi - PK] = gv

    first = [rc(part.at[shard(2 * c + 1 - core)], inc.at[c], s1.at[c], r1.at[c], sib) for c in range(CHIPS)]
    second = [rc(summed.at[c], got.at[chip], s2.at[c], r2.at[chip], (2 * c + core, t_ax)) for c in range(CHIPS)]

    def pass_on(c):
        first[c].wait_recv()
        x = inc[c].astype(F32) + part[shard(2 * c + core), :].astype(F32)
        summed[c] = x.astype(BF)
        pl.when(chip != c)(second[c].start)

    started = 0
    for b in range(PK // 256):
        key_block(b)
        ready = ((b + 1) * 256 // PR) // 2
        for c in range(started, ready):
            first[c].start()
        if b:
            for c in range(passed, started):
                pass_on(c)
        passed, started = started, ready
    for b in range(PK // 256, NK // 256):
        key_block(b)
    for c in range(passed, CHIPS):
        pass_on(c)

    stores = [pltpu.make_async_copy(a, b, os.at[i]) for i, (a, b) in enumerate([
        (dkc, dkc_h), (dvc, dvc_h), (dqp, dqp_h), (dk, dk_h), (dv, dv_h)])]
    stores += [pltpu.make_async_copy(dqc.at[pl.ds(t * 128, 128)], dqc_h.at[pl.ds(t * 128, 128)], os.at[5 + t]) for t in range(NB)]
    stores[0].start()
    stores[1].start()
    for t in range(5):
        n, rws = NKS[t], ROWS[t]
        r0 = t * 1024 if t < NB else RC
        for h in range(0, HEADS, 2):
            a, b = r0 + h * rws, r0 + (h + 2) * rws
            x = dot(DS[a:b, :n], kk[:n]) * RF[a:b, :]
            for j in range(2):
                y = x[j * rws:(j + 1) * rws].astype(BF)
                if t < NB:
                    dqc[t * 128:(t + 1) * 128, (h + j) * D:(h + j + 1) * D] = y
                else:
                    dqp[:, (h + j) * D:(h + j + 1) * D] = y
        stores[5 + t if t < NB else 2].start()

    tot = inc[pl.ds(chip, 1)][0].astype(F32) + part[shard(g), :].astype(F32)
    for j in range(1, CHIPS):
        s = lax.rem(chip + j, CHIPS)
        rc(summed.at[0], got.at[s], s2.at[0], r2.at[s], same[0]).wait_recv()
        tot = tot + got[pl.ds(s, 1)][0].astype(F32)
    dk[...] = tot[:, :D].astype(BF)
    dv[...] = tot[:, D:].astype(BF)
    stores[3].start()
    stores[4].start()
    for c in c1 + c2 + out + fwd + first:
        c.wait_send()
    for c in range(CHIPS):
        pl.when(chip != c)(second[c].wait_send)
    for c in stores:
        c.wait()


def backward(qc, kc, vc, dc, qp, pk, pv, dp, lengths, slot_of, passes):
    hbm = pl.BlockSpec(memory_space=pltpu.HBM)
    dma = lambda n: pltpu.SemaphoreType.DMA((n,))
    b = lambda *s: pltpu.VMEM(s, BF)
    f = lambda *s: pltpu.VMEM(s, F32)
    i = lambda *s: pltpu.VMEM(s, jnp.int32)
    o = lambda *s: jax.ShapeDtypeStruct(s, BF)
    return pl.pallas_call(
        backward_kernel,
        out_shape=(o(CR, 1024), o(CR, D), o(CR, D), o(PR, 1024), o(PR, D), o(PR, D)),
        in_specs=[hbm] * 11, out_specs=[hbm] * 6,
        scratch_shapes=[b(CR, 1024), b(CR, 1024), b(PR, 1024), b(PR, 1024), i(1, 16), i(1, 16), i(1, 4),
                        b(PK, 2 * D), b(CR, D), b(CR, D), b(NK, D), b(2 * D, NK), b(D, NK), b(RA, NK), b(RA, NK), b(D, RA), b(D, RA),
                        f(RA, D), b(HEADS * PR, D), b(HEADS * PR, D),
                        b(CR, 1024), b(PR, 1024), b(CR, D), b(CR, D), b(PR, D), b(PR, D), b(PK, 2 * D),
                        b(CHIPS, PR, 2 * D), b(CHIPS, PR, 2 * D), b(CHIPS, PR, 2 * D), f(8, D), f(NT - 1, 8, D), f(NG, 8, D)]
                       + [f(r, n) for r, n in zip(ROWS, NKS)] * 2
                       + [dma(11), dma(9), dma(2 * CHIPS - 1), dma(2 * CHIPS - 1), dma(NT - 1), dma(NT - 1), dma(NG - 1), dma(NG - 1),
                          dma(CHIPS), dma(CHIPS), dma(CHIPS), dma(CHIPS)],
        compiler_params=pltpu.CompilerParams(collective_id=1, has_side_effects=True, vmem_limit_bytes=63 << 20),
        name="attention_backward",
    )(qc, kc, vc, dc, qp, pk, pv, dp, lengths.reshape(1, 16), slot_of.reshape(1, 16), passes)


def result_kernel(*refs):
    n = len(refs) // 3
    src, dst, buf, (ls, os) = refs[:n], refs[n:2 * n], refs[2 * n:3 * n], refs[3 * n:]
    cuts = [(i, r) for i in range(n) for r in range(0, src[i].shape[0], 128)]
    at = lambda ref, r: ref.at[pl.ds(r, min(128, ref.shape[0] - r))]
    a = [pltpu.make_async_copy(at(src[i], r), at(buf[i], r), ls.at[k]) for k, (i, r) in enumerate(cuts)]
    b = [pltpu.make_async_copy(at(buf[i], r), at(dst[i], r), os.at[k]) for k, (i, r) in enumerate(cuts)]
    for c in a:
        c.start()
    for c, d in zip(a, b):
        c.wait()
        d.start()
    for c in b:
        c.wait()


def results(*xs):
    hbm = pl.BlockSpec(memory_space=pltpu.HBM)
    n = sum(-(-x.shape[0] // 128) for x in xs)
    return pl.pallas_call(
        result_kernel, out_shape=tuple(jax.ShapeDtypeStruct(x.shape, x.dtype) for x in xs),
        in_specs=[hbm] * len(xs), out_specs=[hbm] * len(xs),
        scratch_shapes=[pltpu.VMEM(x.shape, x.dtype) for x in xs] + [pltpu.SemaphoreType.DMA((n,))] * 2, name="write_results",
    )(*xs)


def per_device(*args):
    return results(*backward(*args))


def solution(mesh):
    gt = P("group", "tensor")
    return jax.shard_map(per_device, mesh=mesh, in_specs=(gt,) * 8 + (P(), P(), gt), out_specs=(gt,) * 6, check_vma=False)
```

```python
import jax
import jax.numpy as jnp
from jax import lax
from jax.experimental import pallas as pl
from jax.experimental.pallas import tpu as pltpu
from jax.sharding import PartitionSpec as P

MESH = pl.DeviceIdType.MESH
NG, NT, TESTS, MAXB, BLK = 16, 8, 32, 4, 128
F32, BF = jnp.float32, jnp.bfloat16
HEADS, D, CR, PR, PK = 8, 128, 512, 96, 1536
NB = CR // 128
NK = PK + CR
RC = HEADS * CR
RA = RC + HEADS * PR
SCALE = D ** -0.5
C2 = SCALE * 1.4426950408889634
NKS = [PK + 128 * (i + 1) for i in range(NB)] + [PK]
RP = HEADS * PR
GC = 256
KB = 32
KEYS = 384
CHIPS = NG // 2


def dot_t(a, b):
    return lax.dot_general(a, b, (((1,), (1,)), ((), ())), preferred_element_type=F32)


def dot(a, b):
    return lax.dot_general(a, b, (((1,), (0,)), ((), ())), preferred_element_type=F32)


def backward_kernel(qc_h, kc_h, vc_h, dc_h, qp_h, pk_h, pv_h, dp_h, len_h, slot_h, passes_h,
                    dqc_h, dkc_h, dvc_h, dqp_h, dk_h, dv_h,
                    qc, dc, qp, dp, lens, slots, passes, kv, kc, vc, kk, vv, W, DS, QR, OR, RF, qps, dps, dqs, pos,
                    dqc, dqp, dkc, dvc, dk, dv, part, inc, summed, got, cnt, cnt_in, rew,
                    S0, S1, T0, T1,
                    ls, os, gs, gr, cs, cr, ws, wr, s1, r1, s2, r2):
    S, T = [S0, S1], [T0, T1]
    g, t_ax = lax.axis_index("group"), lax.axis_index("tensor")
    chip, core = g // 2, lax.rem(g, 2)
    same = [(2 * lax.rem(chip + j, CHIPS) + core, t_ax) for j in range(1, CHIPS)]
    sib = (2 * chip + 1 - core, t_ax)
    group = [(lax.rem(g + j, NG), t_ax) for j in range(1, NG)]
    tens = [(g, lax.rem(t_ax + j, NT)) for j in range(1, NT)]

    def rc(src, dst, s, r, d):
        return pltpu.make_async_remote_copy(src_ref=src, dst_ref=dst, send_sem=s, recv_sem=r, device_id=d, device_id_type=MESH)

    def shard(s):
        return pl.ds(pl.multiple_of(s * PR, 32), PR)

    barrier = pltpu.get_barrier_semaphore()
    for d in group + tens:
        pl.semaphore_signal(barrier, inc=1, device_id=d, device_id_type=MESH)
    mine = shard(g)
    loads = [pltpu.make_async_copy(a, b, ls.at[i]) for i, (a, b) in enumerate([
        (pk_h, kv.at[mine, pl.ds(0, D)]), (pv_h, kv.at[mine, pl.ds(D, D)]), (passes_h, passes), (kc_h, kc), (vc_h, vc),
        (len_h, lens), (slot_h, slots), (qc_h, qc), (dc_h, dc), (qp_h, qp), (dp_h, dp)])]
    for c in loads:
        c.start()
    for c in loads[:3]:
        c.wait()
    cnt[...] = jnp.broadcast_to(jnp.sum(passes[...].astype(F32), axis=1, keepdims=True), (8, D))
    pl.semaphore_wait(barrier, len(group) + len(tens))

    c1 = [rc(cnt, cnt_in.at[j], cs.at[j], cr.at[j], tens[j]) for j in range(NT - 1)]
    out = [rc(kv.at[mine], kv.at[mine], gs.at[j], gr.at[j], same[j - 1] if j else sib) for j in range(CHIPS)]
    for c in out + c1:
        c.start()
    for c in loads[3:]:
        c.wait()
    kk[PK:] = kc[...]
    vv[PK:] = vc[...]
    for h in range(HEADS):
        qps[h * PR:(h + 1) * PR] = qp[:, h * D:(h + 1) * D]
        dps[h * PR:(h + 1) * PR] = dp[:, h * D:(h + 1) * D]
    pos[...] = lax.rem(lax.broadcasted_iota(jnp.int32, (8, RP), 1), PR) + g * PR
    for c in c1:
        c.wait_recv()
    total = cnt[...]
    for j in range(NT - 1):
        total = total + cnt_in[j]
    rew[pl.ds(g, 1)] = (total / TESTS)[None]
    c2 = [rc(rew.at[pl.ds(g, 1)], rew.at[pl.ds(g, 1)], ws.at[j], wr.at[j], group[j]) for j in range(NG - 1)]
    for c in c2:
        c.start()
    fwd = []
    for j in range(1, CHIPS):
        out[j].wait_recv()
        rows = shard(2 * lax.rem(chip - j + CHIPS, CHIPS) + core)
        f = rc(kv.at[rows], kv.at[rows], gs.at[CHIPS - 1 + j], gr.at[CHIPS - 1 + j], sib)
        f.start()
        fwd.append(f)
    out[0].wait_recv()
    for f in fwd:
        f.wait_recv()
    kk[:PK] = kv[:, :D]
    vv[:PK] = kv[:, D:]

    def cols(h):
        return pl.ds(pl.multiple_of(h * D, D), D)

    def group_cols(t, p):
        return pl.ds(pl.multiple_of(t * 1024 + p * GC, GC), GC)

    def qo(t, p):
        if t == NB:
            return qps[p * GC:(p + 1) * GC], dps[p * GC:(p + 1) * GC]
        sl = slice(t * 128, (t + 1) * 128)
        a, b = cols(2 * p), cols(2 * p + 1)
        return jnp.concatenate([qc[sl, a], qc[sl, b]], axis=0), jnp.concatenate([dc[sl, a], dc[sl, b]], axis=0)

    zs = lambda u: u // 8
    zl = lambda u: (u + 1) // 9

    def products(t, p, u, slot):
        n = NKS[t]
        q, o = qo(t, p)
        xs = q.astype(F32) * C2
        hi = xs.astype(BF)
        ql = jnp.concatenate([hi, (xs - hi.astype(F32)).astype(BF)], axis=1)

        def piece(a, b):
            ka = kk[a:b]
            s = dot_t(jnp.concatenate([ka, ka], axis=1), ql)
            if t == NB:
                k = lax.broadcasted_iota(jnp.int32, s.shape, 0) + a
                s = jnp.where(k <= pos[:1, p * GC:(p + 1) * GC], s, -1e30)
            elif b == n:
                k = lax.broadcasted_iota(jnp.int32, (128, GC), 0)
                r = lax.rem(lax.broadcasted_iota(jnp.int32, (128, GC), 1), 128)
                s = jnp.concatenate([s[:b - a - 128], jnp.where(k <= r, s[b - a - 128:], -1e30)], axis=0)
            S[slot][zs(u), a:b] = s
            T[slot][zs(u), a:b] = dot_t(vv[a:b], o)
        cut = [n * i // 3 // 128 * 128 for i in range(3)] + [n]
        return [lambda a=a, b=b: piece(a, b) for a, b in zip(cut[:-1], cut[1:])]

    def softmax(t, p, u, slot):
        n = NKS[t]
        cs = group_cols(t, p) if t < NB else pl.ds(RC + p * GC, GC)
        z = zl(u)
        st = {}

        def top():
            st["m"] = jnp.max(S[slot][z, :n], axis=0, keepdims=True)

        def weights():
            tot = dr = None
            for k in range(0, n, KB):
                e = jnp.exp2(S[slot][z, k:k + KB] - st["m"])
                x = e * T[slot][z, k:k + KB]
                W[k:k + KB, cs] = e.astype(BF)
                a = jnp.sum(e.reshape(KB // 8, 8, GC), axis=0)
                b = jnp.sum(x.reshape(KB // 8, 8, GC), axis=0)
                tot = a if tot is None else tot + a
                dr = b if dr is None else dr + b
            r = 1.0 / jnp.sum(tot, axis=0, keepdims=True)
            st["d"] = jnp.sum(dr, axis=0, keepdims=True) * r
            if t < NB:
                row = lax.rem(lax.broadcasted_iota(jnp.int32, (1, GC), 1), 128) + t * 128
                r = r * jnp.where(row.astype(F32) < live, fac, 0.0)
            RF[:, cs] = jnp.broadcast_to(r * SCALE, (8, GC))
            st["r"] = r

        def grads():
            for k in range(0, n, KB):
                DS[k:k + KB, cs] = (W[k:k + KB, cs].astype(F32) * (T[slot][z, k:k + KB] - st["d"])).astype(BF)
            rt = jnp.transpose(jnp.broadcast_to(st["r"], (D, GC)))
            q, o = qo(t, p)
            QR[cs, :] = (q.astype(F32) * (rt * SCALE)).astype(BF)
            OR[cs, :] = (o.astype(F32) * rt).astype(BF)
        return [top, weights, grads]

    def step(nxt, cur, u, slot):
        a = products(*nxt, u, 1 - slot) if nxt else [lambda: None] * 3
        for f, h in zip(a, softmax(*cur, u, slot)):
            f()
            h()

    for f in products(0, 0, core // 2, 0):
        f()
    for c in c2:
        c.wait_recv()
    center = rew[0]
    for s in range(1, NG):
        center = center + rew[s]
    blocks = jnp.sum(jnp.where(slots[...] == g, lens[...], 0).astype(F32), axis=1, keepdims=True)
    adv = rew[pl.ds(g, 1)][0][:1, :1] - (center / NG)[:1, :1]
    fac = adv * MAXB / blocks
    live = blocks * BLK

    @pl.loop(0, HEADS // 2)
    def _(p):
        for t in range(NB):
            step((t + 1, p) if t < NB - 1 else (0, lax.rem(p + 1, HEADS // 2)), (t, p), p, t % 2)
    for f in products(NB, 0, core // 2, 0):
        f()
    for p in range(RP // GC):
        step((NB, p + 1) if p + 1 < RP // GC else None, (NB, p), core // 2, p % 2)

    def key_block(b):
        lo, hi = b * KEYS, (b + 1) * KEYS
        part[lo:hi, :D] = dot(DS[lo:hi], QR[...]).astype(BF)
        part[lo:hi, D:] = dot(W[lo:hi], OR[...]).astype(BF)

    first = [rc(part.at[shard(2 * c + 1 - core)], inc.at[c], s1.at[c], r1.at[c], sib) for c in range(CHIPS)]
    second = [rc(summed.at[c], got.at[chip], s2.at[c], r2.at[chip], (2 * c + core, t_ax)) for c in range(CHIPS)]

    def pass_on(c):
        first[c].wait_recv()
        x = inc[c].astype(F32) + part[shard(2 * c + core), :].astype(F32)
        summed[c] = x.astype(BF)
        pl.when(chip != c)(second[c].start)

    per = KEYS // (2 * PR)
    for b in range(PK // KEYS):
        key_block(b)
        for c in range(b * per, (b + 1) * per):
            first[c].start()
        for c in range((b - 1) * per, b * per) if b else ():
            pass_on(c)
    for i in range(NB):
        sl = slice(i * 128, (i + 1) * 128)
        rows, cs = slice(PK + i * 128, PK + (i + 1) * 128), slice(i * 1024, RC)
        dkc[sl] = dot(DS[rows, cs], QR[cs]).astype(BF)
        dvc[sl] = dot(W[rows, cs], OR[cs]).astype(BF)
    for c in range(CHIPS - per, CHIPS):
        pass_on(c)

    stores = [pltpu.make_async_copy(a, b, os.at[i]) for i, (a, b) in enumerate([
        (dkc, dkc_h), (dvc, dvc_h), (dqp, dqp_h), (dk, dk_h), (dv, dv_h)])]
    stores += [pltpu.make_async_copy(dqc.at[pl.ds(t * 128, 128)], dqc_h.at[pl.ds(t * 128, 128)], os.at[5 + t]) for t in range(NB)]
    stores[0].start()
    stores[1].start()
    kt = jnp.transpose(kk[...])
    for t in range(NB + 1):
        n = NKS[t]
        for c in range(0, 1024 if t < NB else RP, GC):
            a = t * 1024 + c
            x = jnp.transpose(dot(kt[:, :n], DS[:n, a:a + GC]) * RF[:1, a:a + GC]).astype(BF)
            if t < NB:
                for j in range(2):
                    dqc[t * 128:(t + 1) * 128, c + j * D:c + (j + 1) * D] = x[j * 128:(j + 1) * 128]
            else:
                dqs[c:c + GC] = x
        if t < NB:
            stores[5 + t].start()
    for h in range(HEADS):
        dqp[:, h * D:(h + 1) * D] = dqs[h * PR:(h + 1) * PR]
    stores[2].start()

    tot = inc[pl.ds(chip, 1)][0].astype(F32) + part[shard(g), :].astype(F32)
    for j in range(1, CHIPS):
        s = lax.rem(chip + j, CHIPS)
        rc(summed.at[0], got.at[s], s2.at[0], r2.at[s], same[0]).wait_recv()
        tot = tot + got[pl.ds(s, 1)][0].astype(F32)
    dk[...] = tot[:, :D].astype(BF)
    dv[...] = tot[:, D:].astype(BF)
    stores[3].start()
    stores[4].start()
    for c in c1 + c2 + out + fwd + first:
        c.wait_send()
    for c in range(CHIPS):
        pl.when(chip != c)(second[c].wait_send)
    for c in stores:
        c.wait()


def backward(qc, kc, vc, dc, qp, pk, pv, dp, lengths, slot_of, passes):
    hbm = pl.BlockSpec(memory_space=pltpu.HBM)
    dma = lambda n: pltpu.SemaphoreType.DMA((n,))
    b = lambda *s: pltpu.VMEM(s, BF)
    f = lambda *s: pltpu.VMEM(s, F32)
    i = lambda *s: pltpu.VMEM(s, jnp.int32)
    o = lambda *s: jax.ShapeDtypeStruct(s, BF)
    return pl.pallas_call(
        backward_kernel,
        out_shape=(o(CR, 1024), o(CR, D), o(CR, D), o(PR, 1024), o(PR, D), o(PR, D)),
        in_specs=[hbm] * 11, out_specs=[hbm] * 6,
        scratch_shapes=[b(CR, 1024), b(CR, 1024), b(PR, 1024), b(PR, 1024), i(1, 16), i(1, 16), i(1, 4),
                        b(PK, 2 * D), b(CR, D), b(CR, D), b(NK, D), b(NK, D), b(NK, RA), b(NK, RA), b(RA, D), b(RA, D),
                        f(8, RA), b(RP, D), b(RP, D), b(RP, D), i(8, RP),
                        b(CR, 1024), b(PR, 1024), b(CR, D), b(CR, D), b(PR, D), b(PR, D), b(PK, 2 * D),
                        b(CHIPS, PR, 2 * D), b(CHIPS, PR, 2 * D), b(CHIPS, PR, 2 * D), f(8, D), f(NT - 1, 8, D), f(NG, 8, D)]
                       + [f(1, NK, GC)] * 4
                       + [dma(11), dma(9), dma(2 * CHIPS - 1), dma(2 * CHIPS - 1), dma(NT - 1), dma(NT - 1), dma(NG - 1), dma(NG - 1),
                          dma(CHIPS), dma(CHIPS), dma(CHIPS), dma(CHIPS)],
        compiler_params=pltpu.CompilerParams(collective_id=1, has_side_effects=True, vmem_limit_bytes=63 << 20),
        name="attention_backward",
    )(qc, kc, vc, dc, qp, pk, pv, dp, lengths.reshape(1, 16), slot_of.reshape(1, 16), passes)


def result_kernel(*refs):
    n = len(refs) // 3
    src, dst, buf, (ls, os) = refs[:n], refs[n:2 * n], refs[2 * n:3 * n], refs[3 * n:]
    cuts = [(i, r) for i in range(n) for r in range(0, src[i].shape[0], 128)]
    at = lambda ref, r: ref.at[pl.ds(r, min(128, ref.shape[0] - r))]
    a = [pltpu.make_async_copy(at(src[i], r), at(buf[i], r), ls.at[k]) for k, (i, r) in enumerate(cuts)]
    b = [pltpu.make_async_copy(at(buf[i], r), at(dst[i], r), os.at[k]) for k, (i, r) in enumerate(cuts)]
    for c in a:
        c.start()
    for c, d in zip(a, b):
        c.wait()
        d.start()
    for c in b:
        c.wait()


def results(*xs):
    hbm = pl.BlockSpec(memory_space=pltpu.HBM)
    n = sum(-(-x.shape[0] // 128) for x in xs)
    return pl.pallas_call(
        result_kernel, out_shape=tuple(jax.ShapeDtypeStruct(x.shape, x.dtype) for x in xs),
        in_specs=[hbm] * len(xs), out_specs=[hbm] * len(xs),
        scratch_shapes=[pltpu.VMEM(x.shape, x.dtype) for x in xs] + [pltpu.SemaphoreType.DMA((n,))] * 2, name="write_results",
    )(*xs)


def per_device(*args):
    return results(*backward(*args))


def solution(mesh):
    gt = P("group", "tensor")
    return jax.shard_map(per_device, mesh=mesh, in_specs=(gt,) * 8 + (P(), P(), gt), out_specs=(gt,) * 6, check_vma=False)
```

```python
import jax
import jax.numpy as jnp
from jax import lax
from jax.experimental import pallas as pl
from jax.experimental.pallas import tpu as pltpu
from jax.sharding import PartitionSpec as P

MESH = pl.DeviceIdType.MESH
NG, NT, TESTS, MAXB, BLK = 16, 8, 32, 4, 128
F32, BF = jnp.float32, jnp.bfloat16
HEADS, D, CR, PR, PK = 8, 128, 512, 96, 1536
NB = CR // 128
NK = PK + CR
RC = HEADS * CR
RA = RC + HEADS * PR
SCALE = D ** -0.5
C2 = SCALE * 1.4426950408889634
NKS = [PK + 128 * (i + 1) for i in range(NB)] + [PK]
ROWS = [128] * NB + [PR]
CHIPS = NG // 2


def dot(a, b):
    return lax.dot_general(a, b, (((1,), (0,)), ((), ())), preferred_element_type=F32)


def backward_kernel(qc_h, kc_h, vc_h, dc_h, qp_h, pk_h, pv_h, dp_h, len_h, slot_h, passes_h,
                    dqc_h, dkc_h, dvc_h, dqp_h, dk_h, dv_h,
                    qc, dc, qp, dp, lens, slots, passes, kv, kc, vc, kk, kkt, vt, W, DS, QT, OT, RF, QP, OP,
                    dqc, dqp, dkc, dvc, dk, dv, part, inc, summed, got, cnt, cnt_in, rew,
                    S0, S1, S2, S3, S4, T0, T1, T2, T3, T4,
                    ls, os, gs, gr, cs, cr, ws, wr, s1, r1, s2, r2):
    S, T = [S0, S1, S2, S3, S4], [T0, T1, T2, T3, T4]
    g, t_ax = lax.axis_index("group"), lax.axis_index("tensor")
    chip, core = g // 2, lax.rem(g, 2)
    same = [(2 * lax.rem(chip + j, CHIPS) + core, t_ax) for j in range(1, CHIPS)]
    sib = (2 * chip + 1 - core, t_ax)
    group = [(lax.rem(g + j, NG), t_ax) for j in range(1, NG)]
    tens = [(g, lax.rem(t_ax + j, NT)) for j in range(1, NT)]

    def rc(src, dst, s, r, d):
        return pltpu.make_async_remote_copy(src_ref=src, dst_ref=dst, send_sem=s, recv_sem=r, device_id=d, device_id_type=MESH)

    def shard(s):
        return pl.ds(pl.multiple_of(s * PR, 32), PR)

    barrier = pltpu.get_barrier_semaphore()
    for d in group + tens:
        pl.semaphore_signal(barrier, inc=1, device_id=d, device_id_type=MESH)
    mine = shard(g)
    loads = [pltpu.make_async_copy(a, b, ls.at[i]) for i, (a, b) in enumerate([
        (pk_h, kv.at[mine, pl.ds(0, D)]), (pv_h, kv.at[mine, pl.ds(D, D)]), (passes_h, passes), (kc_h, kc), (vc_h, vc),
        (len_h, lens), (slot_h, slots), (qc_h, qc), (dc_h, dc), (qp_h, qp), (dp_h, dp)])]
    for c in loads:
        c.start()
    for i in range(0, NB, 2):
        z = jnp.zeros((1024, 128), BF)
        W[i * 1024:(i + 1) * 1024, PK + (i + 1) * 128:PK + (i + 2) * 128] = z
        DS[i * 1024:(i + 1) * 1024, PK + (i + 1) * 128:PK + (i + 2) * 128] = z
    for c in loads[:3]:
        c.wait()
    cnt[...] = jnp.broadcast_to(jnp.sum(passes[...].astype(F32), axis=1, keepdims=True), (8, D))
    pl.semaphore_wait(barrier, len(group) + len(tens))

    c1 = [rc(cnt, cnt_in.at[j], cs.at[j], cr.at[j], tens[j]) for j in range(NT - 1)]
    out = [rc(kv.at[mine], kv.at[mine], gs.at[j], gr.at[j], same[j - 1] if j else sib) for j in range(CHIPS)]
    for c in out + c1:
        c.start()
    for c in loads[3:]:
        c.wait()
    kk[PK:] = kc[...]
    kt = jnp.transpose(kc[...])
    kkt[:D, PK:] = kt
    kkt[D:, PK:] = kt
    vt[:, PK:] = jnp.transpose(vc[...])
    for c in c1:
        c.wait_recv()
    total = cnt[...]
    for j in range(NT - 1):
        total = total + cnt_in[j]
    rew[pl.ds(g, 1)] = (total / TESTS)[None]
    c2 = [rc(rew.at[pl.ds(g, 1)], rew.at[pl.ds(g, 1)], ws.at[j], wr.at[j], group[j]) for j in range(NG - 1)]
    for c in c2:
        c.start()
    fwd = []
    for j in range(1, CHIPS):
        out[j].wait_recv()
        rows = shard(2 * lax.rem(chip - j + CHIPS, CHIPS) + core)
        f = rc(kv.at[rows], kv.at[rows], gs.at[CHIPS - 1 + j], gr.at[CHIPS - 1 + j], sib)
        f.start()
        fwd.append(f)
    out[0].wait_recv()
    for f in fwd:
        f.wait_recv()
    kp = kv[:, :D]
    kk[:PK] = kp
    kt = jnp.transpose(kp)
    kkt[:D, :PK] = kt
    kkt[D:, :PK] = kt
    vt[:, :PK] = jnp.transpose(kv[:, D:])

    def cols(h):
        return pl.ds(pl.multiple_of(h * D, D), D)

    def rows_of(t, h):
        if t < NB:
            return pl.multiple_of(t * 1024 + h * 128, 128)
        return pl.multiple_of(RC + h * PR, 32)

    def qo(t, h):
        c = cols(h)
        if t < NB:
            return qc[t * 128:(t + 1) * 128, c], dc[t * 128:(t + 1) * 128, c]
        return qp[:, c], dp[:, c]

    def products(t, h):
        q, o = qo(t, h)
        n = NKS[t]
        xs = q.astype(F32) * C2
        hi = xs.astype(BF)
        lo = (xs - hi.astype(F32)).astype(BF)
        s = dot(jnp.concatenate([hi, lo], axis=1), kkt[:, :n])
        if t < NB:
            r = lax.broadcasted_iota(jnp.int32, (128, 128), 0)
            k = lax.broadcasted_iota(jnp.int32, (128, 128), 1)
            s = jnp.concatenate([s[:, :n - 128], jnp.where(k <= r, s[:, n - 128:], -1e30)], axis=1)
        else:
            r = lax.broadcasted_iota(jnp.int32, s.shape, 0) + g * PR
            k = lax.broadcasted_iota(jnp.int32, s.shape, 1)
            s = jnp.where(k <= r, s, -1e30)
        S[t][...] = s
        T[t][...] = dot(o, vt[:, :n])

    products(0, 0)
    blocks = jnp.sum(jnp.where(slots[...] == g, lens[...], 0).astype(F32), axis=1, keepdims=True)
    live = blocks * BLK

    def softmax(t, h):
        n = NKS[t]
        rr = rows_of(t, h)
        s = S[t][...]
        m = jnp.max(s, axis=1, keepdims=True)
        e = jnp.exp2(s - m)
        tot = jnp.sum(e, axis=1, keepdims=True)
        d = T[t][...]
        r = 1.0 / tot
        drift = jnp.sum(e * d, axis=1, keepdims=True) * r
        out = pl.ds(rr, ROWS[t])
        W[out, :n] = e.astype(BF)
        DS[out, :n] = (e * (d - drift)).astype(BF)
        if t < NB:
            row = lax.broadcasted_iota(jnp.int32, (128, D), 0) + t * 128
            r = r * jnp.where(row.astype(F32) < live, 1.0, 0.0)
        else:
            r = jnp.broadcast_to(r, (PR, D))
        RF[out, :] = r * SCALE
        q, o = qo(t, h)
        qs = (q.astype(F32) * (r * SCALE)).astype(BF)
        os_ = (o.astype(F32) * r).astype(BF)
        if t < NB:
            c = pl.ds(rr, 128)
            QT[:, c] = jnp.transpose(qs)
            OT[:, c] = jnp.transpose(os_)
        else:
            c = pl.ds(rr - RC, PR)
            QP[c, :] = qs
            OP[c, :] = os_

    @pl.loop(0, HEADS)
    def _(h):
        for t in range(5):
            if t < 4:
                products(t + 1, h)
            else:
                products(0, lax.rem(h + 1, HEADS))
            softmax(t, h)
    QT[:, RC:] = jnp.transpose(QP[...])
    OT[:, RC:] = jnp.transpose(OP[...])

    for c in c2:
        c.wait_recv()
    center = rew[0]
    for s in range(1, NG):
        center = center + rew[s]
    adv = rew[pl.ds(g, 1)][0][:1] - (center / NG)[:1]
    fac = adv * MAXB / blocks

    def key_block(b):
        lo, hi = b * 256, (b + 1) * 256
        r0 = 0 if lo < PK else ((lo - PK) // 128) * 1024
        f = jnp.concatenate([fac, fac], axis=1)
        gv = dot(OT[:, r0:RC], W[r0:RC, lo:hi]) * f
        gk = dot(QT[:, r0:RC], DS[r0:RC, lo:hi]) * f
        if lo < PK:
            gv = gv + dot(OT[:, RC:], W[RC:, lo:hi])
            gk = gk + dot(QT[:, RC:], DS[RC:, lo:hi])
        gv, gk = jnp.transpose(gv).astype(BF), jnp.transpose(gk).astype(BF)
        if lo < PK:
            part[lo:hi, :D] = gk
            part[lo:hi, D:] = gv
        else:
            dkc[lo - PK:hi - PK] = gk
            dvc[lo - PK:hi - PK] = gv

    first = [rc(part.at[shard(2 * c + 1 - core)], inc.at[c], s1.at[c], r1.at[c], sib) for c in range(CHIPS)]
    second = [rc(summed.at[c], got.at[chip], s2.at[c], r2.at[chip], (2 * c + core, t_ax)) for c in range(CHIPS)]

    def pass_on(c):
        first[c].wait_recv()
        x = inc[c].astype(F32) + part[shard(2 * c + core), :].astype(F32)
        summed[c] = x.astype(BF)
        pl.when(chip != c)(second[c].start)

    started = 0
    for b in range(PK // 256):
        key_block(b)
        ready = ((b + 1) * 256 // PR) // 2
        for c in range(started, ready):
            first[c].start()
        if b:
            for c in range(passed, started):
                pass_on(c)
        passed, started = started, ready
    for b in range(PK // 256, NK // 256):
        key_block(b)
    for c in range(passed, CHIPS):
        pass_on(c)

    stores = [pltpu.make_async_copy(a, b, os.at[i]) for i, (a, b) in enumerate([
        (dkc, dkc_h), (dvc, dvc_h), (dqp, dqp_h), (dk, dk_h), (dv, dv_h)])]
    stores += [pltpu.make_async_copy(dqc.at[pl.ds(t * 128, 128)], dqc_h.at[pl.ds(t * 128, 128)], os.at[5 + t]) for t in range(NB)]
    stores[0].start()
    stores[1].start()
    for t in range(5):
        n, rws = NKS[t], ROWS[t]
        r0 = t * 1024 if t < NB else RC
        for h in range(0, HEADS, 2):
            a, b = r0 + h * rws, r0 + (h + 2) * rws
            x = dot(DS[a:b, :n], kk[:n]) * (RF[a:b, :] * fac if t < NB else RF[a:b, :])
            for j in range(2):
                y = x[j * rws:(j + 1) * rws].astype(BF)
                if t < NB:
                    dqc[t * 128:(t + 1) * 128, (h + j) * D:(h + j + 1) * D] = y
                else:
                    dqp[:, (h + j) * D:(h + j + 1) * D] = y
        stores[5 + t if t < NB else 2].start()

    tot = inc[pl.ds(chip, 1)][0].astype(F32) + part[shard(g), :].astype(F32)
    for j in range(1, CHIPS):
        s = lax.rem(chip + j, CHIPS)
        rc(summed.at[0], got.at[s], s2.at[0], r2.at[s], same[0]).wait_recv()
        tot = tot + got[pl.ds(s, 1)][0].astype(F32)
    dk[...] = tot[:, :D].astype(BF)
    dv[...] = tot[:, D:].astype(BF)
    stores[3].start()
    stores[4].start()
    for c in c1 + c2 + out + fwd + first:
        c.wait_send()
    for c in range(CHIPS):
        pl.when(chip != c)(second[c].wait_send)
    for c in stores:
        c.wait()


def backward(qc, kc, vc, dc, qp, pk, pv, dp, lengths, slot_of, passes):
    hbm = pl.BlockSpec(memory_space=pltpu.HBM)
    dma = lambda n: pltpu.SemaphoreType.DMA((n,))
    b = lambda *s: pltpu.VMEM(s, BF)
    f = lambda *s: pltpu.VMEM(s, F32)
    i = lambda *s: pltpu.VMEM(s, jnp.int32)
    o = lambda *s: jax.ShapeDtypeStruct(s, BF)
    return pl.pallas_call(
        backward_kernel,
        out_shape=(o(CR, 1024), o(CR, D), o(CR, D), o(PR, 1024), o(PR, D), o(PR, D)),
        in_specs=[hbm] * 11, out_specs=[hbm] * 6,
        scratch_shapes=[b(CR, 1024), b(CR, 1024), b(PR, 1024), b(PR, 1024), i(1, 16), i(1, 16), i(1, 4),
                        b(PK, 2 * D), b(CR, D), b(CR, D), b(NK, D), b(2 * D, NK), b(D, NK), b(RA, NK), b(RA, NK), b(D, RA), b(D, RA),
                        f(RA, D), b(HEADS * PR, D), b(HEADS * PR, D),
                        b(CR, 1024), b(PR, 1024), b(CR, D), b(CR, D), b(PR, D), b(PR, D), b(PK, 2 * D),
                        b(CHIPS, PR, 2 * D), b(CHIPS, PR, 2 * D), b(CHIPS, PR, 2 * D), f(8, D), f(NT - 1, 8, D), f(NG, 8, D)]
                       + [f(r, n) for r, n in zip(ROWS, NKS)] * 2
                       + [dma(11), dma(9), dma(2 * CHIPS - 1), dma(2 * CHIPS - 1), dma(NT - 1), dma(NT - 1), dma(NG - 1), dma(NG - 1),
                          dma(CHIPS), dma(CHIPS), dma(CHIPS), dma(CHIPS)],
        compiler_params=pltpu.CompilerParams(collective_id=1, has_side_effects=True, vmem_limit_bytes=63 << 20),
        name="attention_backward",
    )(qc, kc, vc, dc, qp, pk, pv, dp, lengths.reshape(1, 16), slot_of.reshape(1, 16), passes)


def result_kernel(*refs):
    n = len(refs) // 3
    src, dst, buf, (ls, os) = refs[:n], refs[n:2 * n], refs[2 * n:3 * n], refs[3 * n:]
    cuts = [(i, r) for i in range(n) for r in range(0, src[i].shape[0], 128)]
    at = lambda ref, r: ref.at[pl.ds(r, min(128, ref.shape[0] - r))]
    a = [pltpu.make_async_copy(at(src[i], r), at(buf[i], r), ls.at[k]) for k, (i, r) in enumerate(cuts)]
    b = [pltpu.make_async_copy(at(buf[i], r), at(dst[i], r), os.at[k]) for k, (i, r) in enumerate(cuts)]
    for c in a:
        c.start()
    for c, d in zip(a, b):
        c.wait()
        d.start()
    for c in b:
        c.wait()


def results(*xs):
    hbm = pl.BlockSpec(memory_space=pltpu.HBM)
    n = sum(-(-x.shape[0] // 128) for x in xs)
    return pl.pallas_call(
        result_kernel, out_shape=tuple(jax.ShapeDtypeStruct(x.shape, x.dtype) for x in xs),
        in_specs=[hbm] * len(xs), out_specs=[hbm] * len(xs),
        scratch_shapes=[pltpu.VMEM(x.shape, x.dtype) for x in xs] + [pltpu.SemaphoreType.DMA((n,))] * 2, name="write_results",
    )(*xs)


def per_device(*args):
    return results(*backward(*args))


def solution(mesh):
    gt = P("group", "tensor")
    return jax.shard_map(per_device, mesh=mesh, in_specs=(gt,) * 8 + (P(), P(), gt), out_specs=(gt,) * 6, check_vma=False)
```
